256 devices in a mesh: section: 16 (over z, core), dp: 16 (over x, y).
Axes of the slice: x: 4, y: 4, z: 8, core: 2. Of those that a mesh axis runs over, the one named last changes fastest.
Arguments:
- layer_input: bfloat16 [16, 4096, 8192], P('section', 'dp'), may hold values from -6 to 6
- key_cotangent: bfloat16 [16, 4096, 1024], P('section', 'dp'), may hold values from -6 to 6
- key_weight: bfloat16 [16, 8192, 1024], P('section', 'dp'), may hold values from -0.09375 to 0.09375
- block_mask: int32 [16, 128, 16], P('section'), may hold values from 0 to 1, as said below
Outputs:
- key_grad: float32 [16, 8192, 1024], P('section', 'dp')
- input_grad: bfloat16 [16, 4096, 8192], P('section', 'dp')
The draws below stay inside these ranges and needn't reach their ends.
Inputs may be any that keep to these rules, and one draw needn't show every extreme that they name: `block_mask`: in each layer every aligned group of 8 block rows holds 2, 4 or 6 times 1024 / 64 kept blocks, and some group holds exactly 96.
All inputs are finite; a program needn't handle non-finite values.
Results may differ from the reference program's by a relative error of at most 0.001.
Values may be sent and summed in bfloat16 or wider, within the bound.
No kernel may reach another device: no remote copies, remote signals or barrier semaphores. Data moves between devices by JAX's collectives and lax.ppermute only.
A program may use at most 320 MiB of HBM per device.

```python
import math
import jax
import jax.numpy as jnp
from jax import lax

D = 8192
KV = 1024
BLOCK = 64
GROUP_ROWS = 8
TOKENS = 4096
LAYERS = 16


def draw_block_mask(key, part):
    key = jax.random.fold_in(key, 7)
    groups = D // BLOCK // GROUP_ROWS
    block_cols = KV // BLOCK
    slots = GROUP_ROWS * block_cols
    key_level, key_forced, key_score = jax.random.split(key, 3)
    levels = jax.random.randint(key_level, (LAYERS, groups), 1, 4)
    forced = jax.random.randint(key_forced, (LAYERS, 1), 0, groups)
    levels = jnp.where(jnp.arange(groups)[None, :] == forced, 3, levels)
    counts = levels * 2 * block_cols
    scores = jax.random.randint(key_score, (LAYERS, groups, slots), 0, 1 << 20) * slots + jnp.arange(slots)[None, None, :]
    ranks = jnp.argsort(jnp.argsort(scores, axis=-1), axis=-1)
    flags = (ranks < counts[:, :, None]).astype(jnp.int32)
    return flags.reshape(LAYERS, D // BLOCK, block_cols)


def raised(array, key, source, target, shards_of, factor):
    def block_of(dim):
        return (jnp.arange(array.shape[dim]) // (array.shape[dim] // shards_of)).reshape((-1,) + (1,) * (array.ndim - 1 - dim))

    near = jax.random.permutation(key, shards_of)[block_of(target)]
    second = (block_of(target) + shards_of // 2) % shards_of
    return jnp.where((block_of(source) == near) | (block_of(source) == second), factor * array, array)


def block_levels(own_key, extent, cuts, low, top_value):
    def one(dim, blocks):
        draws = jax.random.uniform(jax.random.fold_in(jax.random.fold_in(own_key, 6), dim), (blocks,), jnp.float32, low / len(cuts), top_value / len(cuts))
        return jnp.repeat(jnp.exp(draws), extent[dim] // blocks).reshape((-1,) + (1,) * (len(extent) - dim - 1))

    loudness = one(*cuts[0])
    for cut in cuts[1:]:
        loudness = loudness * one(*cut)
    return loudness


def bell_draw(rng, extent, spread, bound, shards=(), kind=jnp.bfloat16):
    entries = jax.random.normal(rng, extent, jnp.float32) * spread
    if len(shards) > 0:
        entries = block_levels(rng, extent, shards, -0.22, 0.18) * entries
    return jnp.clip(entries, min=-bound, max=bound).astype(kind)


def noise_with(key, shape, deviation, reach, cuts, heavy, kind=jnp.bfloat16):
    values = deviation * jax.random.normal(key, shape, jnp.float32)
    if cuts:
        values = values * block_levels(key, shape, cuts, -0.22, 0.18)
    return jnp.clip(raised(values, jax.random.fold_in(key, 3), *heavy), -reach, reach).astype(kind)


def setup_inputs(seed: int = 0) -> dict:
    streams_of = jax.random.split(jax.random.key(seed), 5)
    return {
        "layer_input": noise_with(streams_of[0], (LAYERS, TOKENS, D), 1.0, 6.0, ((0, 16), (1, 16)), (1, 2, 16, 2.0)),
        "key_cotangent": bell_draw(streams_of[1], (LAYERS, TOKENS, KV), 1.0, 6.0, ((0, 16), (1, 16))),
        "key_weight": bell_draw(streams_of[2], (LAYERS, D, KV), (D // 2) ** -0.5, 0.09375, ((0, 16), (1, 16))),
        "block_mask": draw_block_mask(jax.random.fold_in(streams_of[4], 71), 0),
    }


def expand(flags):
    return jnp.repeat(jnp.repeat(flags, BLOCK, 0), BLOCK, 1)

def reference(layer_input, key_cotangent, key_weight, block_mask):
    grad_scale = 1.0 / math.sqrt(TOKENS)

    def layer_backward(items):
        inputs, cotangent, weight, flags_layer = items
        element_mask = expand(flags_layer)
        masked = weight * element_mask.astype(weight.dtype)
        layer_grad = lax.dot_general(cotangent, masked, (((1,), (1,)), ((), ())), preferred_element_type=jnp.float32).astype(jnp.bfloat16)
        weight_grad = lax.dot_general(inputs, cotangent, (((0,), (0,)), ((), ())), preferred_element_type=jnp.float32)
        weight_grad = weight_grad * element_mask.astype(jnp.float32) * grad_scale
        return (layer_grad, weight_grad)
    layer_grad, key_grad = lax.map(layer_backward, (layer_input, key_cotangent, key_weight, block_mask))
    input_grad = jnp.concatenate([layer_grad[1:], jnp.zeros_like(layer_grad[:1])], 0)
    return (key_grad, input_grad)
```

```python
import math

import jax
import jax.numpy as jnp
from jax import lax
from jax.experimental import pallas as pl
from jax.experimental.pallas import tpu as pltpu
from jax.sharding import PartitionSpec as P

BLOCK = 64
SIDE = 4


def along_x(value, steps):
    return lax.ppermute(
        value,
        "dp",
        [
            (x * SIDE + y, (x + steps) % SIDE * SIDE + y)
            for x in range(SIDE)
            for y in range(SIDE)
        ],
    )


def along_y(value, steps):
    return lax.ppermute(
        value,
        "dp",
        [
            (x * SIDE + y, x * SIDE + (y + steps) % SIDE)
            for x in range(SIDE)
            for y in range(SIDE)
        ],
    )


def to_layer_below(value):
    count = lax.axis_size("section")
    return lax.ppermute(value, "section", [(s, s - 1) for s in range(1, count)])


def expand(flags):
    return jnp.repeat(jnp.repeat(flags, BLOCK, 0), BLOCK, 1)


def column_start(place_ref, k, m, half, width):
    x = lax.rem(place_ref[0] + k, SIDE)
    y = lax.rem(place_ref[1] + m, SIDE)
    return pl.multiple_of((x * SIDE + y) * (2 * width) + half * width, width)


def run_copies(copies):
    for copy in copies:
        copy.start()
    for copy in copies:
        copy.wait()


def split_kernel(place_ref, whole_ref, *refs):
    pieces, sems = refs[: 2 * SIDE], refs[2 * SIDE]
    width = pieces[0].shape[1] // SIDE
    copies = []
    for a in range(SIDE):
        for b in range(SIDE):
            for half in range(2):
                k, m = (a, b) if half == 0 else (b, a)
                copies.append(
                    pltpu.make_async_copy(
                        whole_ref.at[:, pl.ds(column_start(place_ref, k, m, half, width), width)],
                        pieces[half * SIDE + a].at[:, pl.ds(b * width, width)],
                        sems.at[len(copies)],
                    )
                )
    run_copies(copies)


def join_kernel(place_ref, *refs):
    pieces, whole_ref, sems = refs[: 2 * SIDE], refs[2 * SIDE], refs[2 * SIDE + 1]
    width = pieces[0].shape[1] // SIDE
    copies = []
    for a in range(SIDE):
        for b in range(SIDE):
            for half in range(2):
                k, m = (a, b) if half == 0 else (b, a)
                copies.append(
                    pltpu.make_async_copy(
                        pieces[half * SIDE + a].at[:, pl.ds(b * width, width)],
                        whole_ref.at[:, pl.ds(column_start(place_ref, k, m, half, width), width)],
                        sems.at[len(copies)],
                    )
                )
    run_copies(copies)


def split_columns(place, whole):
    rows, columns = whole.shape
    piece = jax.ShapeDtypeStruct((rows, columns // (2 * SIDE)), whole.dtype)
    return pl.pallas_call(
        split_kernel,
        out_shape=[piece] * (2 * SIDE),
        in_specs=[pl.BlockSpec(memory_space=pltpu.SMEM), pl.BlockSpec(memory_space=pl.ANY)],
        out_specs=[pl.BlockSpec(memory_space=pl.ANY)] * (2 * SIDE),
        scratch_shapes=[pltpu.SemaphoreType.DMA((2 * SIDE * SIDE,))],
        cost_estimate=pl.CostEstimate(flops=0, bytes_accessed=4 * rows * columns, transcendentals=0),
    )(place, whole)


def join_columns(place, pieces):
    rows, columns = pieces[0].shape
    return pl.pallas_call(
        join_kernel,
        out_shape=jax.ShapeDtypeStruct((rows, columns * 2 * SIDE), pieces[0].dtype),
        in_specs=[pl.BlockSpec(memory_space=pltpu.SMEM)]
        + [pl.BlockSpec(memory_space=pl.ANY)] * (2 * SIDE),
        out_specs=pl.BlockSpec(memory_space=pl.ANY),
        scratch_shapes=[pltpu.SemaphoreType.DMA((2 * SIDE * SIDE,))],
        cost_estimate=pl.CostEstimate(
            flops=0, bytes_accessed=4 * rows * columns * 2 * SIDE, transcendentals=0
        ),
    )(place, *pieces)


def gather_line(move, cotangent, rows):
    tokens = cotangent.shape[0]
    both = jnp.concatenate([cotangent, rows], 0)
    before = move(both, 1)
    after = move(both, -1)
    far_cotangent = move(before[:tokens], 1)
    far_rows = move(after[tokens:], -1)
    return (
        [cotangent, after[:tokens], far_cotangent, before[:tokens]],
        [rows, after[tokens:], far_rows, before[tokens:]],
        before,
    )


def shards(layer_input, key_cotangent, key_weight, block_mask):
    inputs = layer_input[0]
    cotangent = key_cotangent[0]
    weight = key_weight[0]
    flags_layer = block_mask[0]
    own_index = lax.axis_index("dp")
    row_count = weight.shape[0]
    half = row_count // 2
    block_rows = row_count // BLOCK
    place = jnp.stack([own_index // SIDE, own_index % SIDE]).astype(jnp.int32)

    own_flags = lax.dynamic_slice_in_dim(flags_layer, own_index * block_rows, block_rows, 0)
    masked = weight * expand(own_flags).astype(weight.dtype)

    cot_x, rows_x, seen_x = gather_line(along_x, cotangent, masked[half:])
    cot_y, rows_y, seen_y = gather_line(along_y, cotangent, masked[:half])

    inputs, _, _ = lax.optimization_barrier((inputs, seen_x, seen_y))
    pieces = split_columns(place, inputs)
    in_x = [pieces[0]] + [along_x(pieces[-j % SIDE], -j) for j in range(1, SIDE)]
    in_y = [pieces[SIDE]] + [along_y(pieces[SIDE + -j % SIDE], -j) for j in range(1, SIDE)]

    def layer_term(cot, rows):
        rows = jnp.concatenate(rows, 0)
        return [
            lax.dot_general(
                c, rows, (((1,), (1,)), ((), ())), preferred_element_type=jnp.float32
            ).astype(jnp.bfloat16)
            for c in cot
        ]

    out_x = layer_term(cot_x, rows_y)
    out_y = layer_term(cot_y, rows_x)
    grad_x = [out_x[0]] + [along_x(out_x[-j % SIDE], -j) for j in range(1, SIDE)]
    grad_y = [out_y[0]] + [along_y(out_y[-j % SIDE], -j) for j in range(1, SIDE)]
    incoming = [to_layer_below(piece) for piece in grad_x + grad_y]
    input_grad = join_columns(place, incoming)

    def weight_term(ins, cot):
        ins = jnp.concatenate(ins, 0)
        cot = jnp.concatenate(cot, 0)
        return [
            lax.dot_general(
                ins[:, half * m : half * (m + 1)],
                cot,
                (((0,), (0,)), ((), ())),
                preferred_element_type=jnp.float32,
            )
            for m in range(SIDE)
        ]

    part_x = weight_term(in_x, cot_x)
    part_y = weight_term(in_y, cot_y)
    top = part_x[0] + sum(along_y(part_x[-j % SIDE], -j) for j in range(1, SIDE))
    bottom = part_y[0] + sum(along_x(part_y[-j % SIDE], -j) for j in range(1, SIDE))
    grad_scale = 1.0 / math.sqrt(cotangent.shape[0] * lax.axis_size("dp"))
    weight_grad = jnp.concatenate([top, bottom], 0) * (
        expand(own_flags).astype(jnp.float32) * grad_scale
    )
    return (weight_grad[None], input_grad[None])


def solution(mesh):
    placed = (
        P("section", "dp", None),
        P("section", "dp", None),
        P("section", "dp", None),
        P("section", None, None),
    )
    return jax.shard_map(
        shards,
        mesh=mesh,
        in_specs=placed,
        out_specs=(P("section", "dp", None), P("section", "dp", None)),
        check_vma=False,
    )
```

```python
import math

import jax
import jax.numpy as jnp
from jax import lax
from jax.experimental import pallas as pl
from jax.experimental.pallas import tpu as pltpu
from jax.sharding import PartitionSpec as P

BLOCK = 64
SIDE = 4
TAIL = 8


def on_axis(index, parity, first, steps):
    x, y = index // SIDE, index % SIDE
    if (parity == 0) == first:
        x = (x + steps) % SIDE
    else:
        y = (y + steps) % SIDE
    return x * SIDE + y


def move(value, first, steps):
    sections, replicas = lax.axis_size("section"), lax.axis_size("dp")
    pairs = [
        (s * replicas + i, s * replicas + on_axis(i, s % 2, first, steps))
        for s in range(sections)
        for i in range(replicas)
    ]
    return lax.ppermute(value, ("section", "dp"), pairs)


def to_layer_below(value):
    count = lax.axis_size("section")
    return lax.ppermute(value, "section", [(s, s - 1) for s in range(1, count)])


def expand(flags):
    return jnp.repeat(jnp.repeat(flags, BLOCK, 0), BLOCK, 1)


def column_start(place_ref, k, m, width):
    a = lax.rem(place_ref[1] + k, SIDE)
    b = lax.rem(place_ref[2] + m, SIDE)
    owner = jnp.where(place_ref[0] == 0, a * SIDE + b, b * SIDE + a)
    return pl.multiple_of(owner * width, width)


def split_kernel(place_ref, whole_ref, *pieces):
    width = pieces[0].shape[1] // SIDE
    for k in range(SIDE):
        for m in range(SIDE):
            start = column_start(place_ref, k, m, width)
            pieces[k][:, m * width : (m + 1) * width] = whole_ref[:, pl.ds(start, width)]


def join_kernel(place_ref, *refs):
    pieces, whole_ref = refs[:SIDE], refs[SIDE]
    width = pieces[0].shape[1] // SIDE
    for k in range(SIDE):
        for m in range(SIDE):
            start = column_start(place_ref, k, m, width)
            whole_ref[:, pl.ds(start, width)] = pieces[k][:, m * width : (m + 1) * width]


def layer_kernel(*refs):
    cots, rows, outs = refs[:SIDE], refs[SIDE : 2 * SIDE], refs[2 * SIDE :]
    width = rows[0].shape[0]
    for m in range(SIDE):
        for j in range(SIDE):
            outs[j][:, m * width : (m + 1) * width] = lax.dot_general(
                cots[j][...],
                rows[m][...],
                (((1,), (1,)), ((), ())),
                preferred_element_type=jnp.float32,
            ).astype(jnp.bfloat16)


def weight_kernel(*refs):
    ins, cots = refs[:SIDE], refs[SIDE : 2 * SIDE]
    outs, exponent_ref = refs[2 * SIDE : 3 * SIDE], refs[3 * SIDE]
    width = outs[0].shape[0]
    cot = jnp.concatenate([c[...] for c in cots], 0)
    for m in range(SIDE):
        part = lax.dot_general(
            jnp.concatenate([i[:, m * width : (m + 1) * width] for i in ins], 0),
            cot,
            (((0,), (0,)), ((), ())),
            preferred_element_type=jnp.float32,
        )
        outs[m][...] = part
        if m > 0:
            peak = jnp.max(jnp.abs(part), axis=0, keepdims=True)
            peak = jnp.max(peak, axis=1, keepdims=True)
            exponent = jnp.clip(jnp.floor(14.0 - jnp.log2(peak)), -100.0, 100.0)
            exponent_ref[m - 1 : m, :] = jnp.broadcast_to(exponent, (1, exponent_ref.shape[1]))


def local_call(kernel, out_shape, operands, scalars=0, flops=0):
    shapes = list(operands) + list(out_shape)
    moved = sum(math.prod(a.shape) * a.dtype.itemsize for a in shapes)
    vmem = pl.BlockSpec(memory_space=pltpu.VMEM)
    return pl.pallas_call(
        kernel,
        out_shape=out_shape,
        in_specs=[pl.BlockSpec(memory_space=pltpu.SMEM)] * scalars
        + [vmem] * (len(operands) - scalars),
        out_specs=[vmem] * len(out_shape),
        compiler_params=pltpu.CompilerParams(vmem_limit_bytes=40 * 1024 * 1024),
        cost_estimate=pl.CostEstimate(flops=flops, bytes_accessed=moved, transcendentals=0),
    )(*operands)


def split_columns(place, whole):
    rows, columns = whole.shape
    piece = jax.ShapeDtypeStruct((rows, columns // SIDE), whole.dtype)
    return local_call(split_kernel, [piece] * SIDE, [place, whole], 1)


def join_columns(place, pieces):
    rows, columns = pieces[0].shape
    whole = jax.ShapeDtypeStruct((rows, columns * SIDE), pieces[0].dtype)
    return local_call(join_kernel, [whole], [place, *pieces], 1)[0]


def layer_terms(cots, rows):
    tokens, features = cots[0].shape
    width = rows[0].shape[0]
    out = jax.ShapeDtypeStruct((tokens, SIDE * width), jnp.bfloat16)
    flops = 2 * tokens * features * width * SIDE * SIDE
    return local_call(layer_kernel, [out] * SIDE, [*cots, *rows], 0, flops)


def weight_terms(ins, cots):
    tokens, features = cots[0].shape
    width = ins[0].shape[1] // SIDE
    part = jax.ShapeDtypeStruct((width, features), jnp.float32)
    exponents = jax.ShapeDtypeStruct((SIDE - 1, 128), jnp.float32)
    flops = 2 * tokens * features * width * SIDE * SIDE
    *parts, exponents = local_call(
        weight_kernel, [part] * SIDE + [exponents], [*ins, *cots], 0, flops
    )
    return parts, exponents[:, 0]


def exchange(pieces, first):
    return [pieces[0]] + [move(pieces[-j % SIDE], first, -j) for j in range(1, SIDE)]


def gather(value, first):
    return exchange([value] * SIDE, first)


def coded(part, exponent):
    tail = jnp.full((TAIL, part.shape[1]), exponent)
    return jnp.concatenate([part * jnp.exp2(exponent), tail], 0).astype(jnp.float16)


def decoded(value):
    value = value.astype(jnp.float32)
    return value[:-TAIL] * jnp.exp2(-value[-1:, :1])


def shards(layer_input, key_cotangent, key_weight, block_mask):
    inputs = layer_input[0]
    cotangent = key_cotangent[0]
    weight = key_weight[0]
    flags_layer = block_mask[0]
    own_index = lax.axis_index("dp")
    parity = lax.axis_index("section") % 2
    x, y = own_index // SIDE, own_index % SIDE
    block_rows = weight.shape[0] // BLOCK
    even = jnp.stack([0, x, y]).astype(jnp.int32)
    odd = jnp.stack([1, y, x]).astype(jnp.int32)
    place = jnp.where(parity == 0, even, odd)
    place_above = jnp.where(parity == 0, odd, even)

    with jax.named_scope("cot"):
        cots = gather(cotangent, True)

    with jax.named_scope("rows"):
        own_flags = lax.dynamic_slice_in_dim(flags_layer, own_index * block_rows, block_rows, 0)
        masked = weight * expand(own_flags).astype(weight.dtype)
        rows = gather(masked, False)

    with jax.named_scope("ins"):
        inputs, _ = lax.optimization_barrier((inputs, rows[1]))
        ins = exchange(split_columns(place, inputs), True)

    with jax.named_scope("layer"):
        grads = exchange(layer_terms(cots, rows), True)
    with jax.named_scope("below"):
        incoming = [to_layer_below(piece) for piece in grads]
        input_grad = join_columns(place_above, incoming)

    with jax.named_scope("weight"):
        parts, exponents = weight_terms(ins, cots)
        sent = exchange(
            [parts[0]] + [coded(parts[m], exponents[m - 1]) for m in range(1, SIDE)], False
        )
        total = sent[0] + sum(decoded(value) for value in sent[1:])
        grad_scale = 1.0 / math.sqrt(cotangent.shape[0] * lax.axis_size("dp"))
        weight_grad = total * (expand(own_flags).astype(jnp.float32) * grad_scale)
    return (weight_grad[None], input_grad[None])


def solution(mesh):
    placed = (
        P("section", "dp", None),
        P("section", "dp", None),
        P("section", "dp", None),
        P("section", None, None),
    )
    return jax.shard_map(
        shards,
        mesh=mesh,
        in_specs=placed,
        out_specs=(P("section", "dp", None), P("section", "dp", None)),
        check_vma=False,
    )
```

```python
import functools
import math

import jax
import jax.numpy as jnp
from jax import lax
from jax.experimental import pallas as pl
from jax.experimental.pallas import tpu as pltpu
from jax.sharding import PartitionSpec as P

BLOCK = 64
SIDE = 4
TAIL = 8
VMEM = pl.BlockSpec(memory_space=pltpu.VMEM)
SMEM = pl.BlockSpec(memory_space=pltpu.SMEM)
HBM = pl.BlockSpec(memory_space=pltpu.HBM)


def on_axis(index, parity, first, steps):
    x, y = index // SIDE, index % SIDE
    if (parity == 0) == first:
        x = (x + steps) % SIDE
    else:
        y = (y + steps) % SIDE
    return x * SIDE + y


def move(value, first, steps):
    sections, replicas = lax.axis_size("section"), lax.axis_size("dp")
    pairs = [
        (s * replicas + i, s * replicas + on_axis(i, s % 2, first, steps))
        for s in range(sections)
        for i in range(replicas)
    ]
    return lax.ppermute(value, ("section", "dp"), pairs)


def to_layer_below(value):
    count = lax.axis_size("section")
    return lax.ppermute(value, "section", [(s, s - 1) for s in range(1, count)])


def column_start(place_ref, k, m, width):
    a = lax.rem(place_ref[1] + k, SIDE)
    b = lax.rem(place_ref[2] + m, SIDE)
    owner = jnp.where(place_ref[0] == 0, a * SIDE + b, b * SIDE + a)
    return pl.multiple_of(owner * width, width)


def mask_kernel(place_ref, flags_ref, weight_ref, masked_ref, mask_ref):
    rows, columns = weight_ref.shape
    block_columns, all_block_rows = flags_ref.shape
    first = place_ref[3] * (rows // BLOCK)

    def spread(short, long, offset):
        block = lax.broadcasted_iota(jnp.int32, (short, long), 1) // BLOCK + offset
        return (block == lax.broadcasted_iota(jnp.int32, (short, long), 0)).astype(jnp.float32)

    tall = jnp.dot(
        flags_ref[...].astype(jnp.float32),
        spread(all_block_rows, rows, first),
        preferred_element_type=jnp.float32,
    )
    mask = lax.dot_general(
        tall,
        spread(block_columns, columns, 0),
        (((0,), (0,)), ((), ())),
        preferred_element_type=jnp.float32,
    ).astype(jnp.bfloat16)
    mask_ref[...] = mask
    masked_ref[...] = weight_ref[...] * mask


def split_kernel(place_ref, cot_ref, whole_ref, *refs):
    pieces, sem = refs[:SIDE], refs[SIDE]
    features = cot_ref.shape[1]
    width = (pieces[0].shape[1] - features) // SIDE
    copies = []
    for k in (2, 1, 3, 0):
        for m in range(SIDE):
            start = column_start(place_ref, k, m, width)
            copies.append(
                pltpu.make_async_copy(
                    whole_ref.at[:, pl.ds(start, width)],
                    pieces[k].at[:, pl.ds(m * width, width)],
                    sem.at[k, m],
                )
            )
    for copy in copies:
        copy.start()
    for piece in pieces:
        piece[:, SIDE * width :] = cot_ref[...]
    for copy in copies:
        copy.wait()


def join_kernel(senders, place_ref, *refs):
    pieces, whole_ref, sem = refs[: len(senders)], refs[-2], refs[-1]
    width = pieces[0].shape[1] // SIDE
    copies = []
    for n, m in enumerate(senders):
        for k in range(SIDE):
            start = column_start(place_ref, k, m, width)
            copies.append(
                pltpu.make_async_copy(
                    pieces[n].at[:, pl.ds(k * width, width)],
                    whole_ref.at[:, pl.ds(start, width)],
                    sem.at[n, k],
                )
            )
    for copy in copies:
        copy.start()
    for copy in copies:
        copy.wait()


def layer_kernel(j, cots_ref, *refs):
    rows, out_ref = refs[:-1], refs[-1]
    tokens = out_ref.shape[0]
    start = 0
    for row_ref in rows:
        stop = start + row_ref.shape[0]
        out_ref[:, start:stop] = lax.dot_general(
            cots_ref[j * tokens : (j + 1) * tokens, :],
            row_ref[...],
            (((1,), (1,)), ((), ())),
            preferred_element_type=jnp.float32,
        ).astype(jnp.bfloat16)
        start = stop


def weight_kernel(m, coded, *refs):
    ins, cots_ref, out_ref = refs[:SIDE], refs[SIDE], refs[SIDE + 1]
    features = out_ref.shape[1]
    width = (ins[0].shape[1] - features) // SIDE
    part = lax.dot_general(
        jnp.concatenate([i[:, m * width : (m + 1) * width] for i in ins], 0),
        cots_ref[...],
        (((0,), (0,)), ((), ())),
        preferred_element_type=jnp.float32,
    )
    if coded:
        peak = jnp.max(jnp.abs(part), axis=0, keepdims=True)
        peak = jnp.max(peak, axis=1, keepdims=True)
        exponent = jnp.clip(jnp.floor(14.0 - jnp.log2(peak)), -100.0, 100.0)
        out_ref[:width, :] = part * jnp.exp2(exponent)
        out_ref[width:, :] = jnp.broadcast_to(exponent, (TAIL, features))
    else:
        out_ref[...] = part


def local_call(
    kernel, out_shape, operands, in_specs, out_specs, scratch=(), flops=0, aliases={}, mib=40
):
    shapes = list(operands) + list(out_shape)
    moved = sum(math.prod(a.shape) * a.dtype.itemsize for a in shapes)
    return pl.pallas_call(
        kernel,
        out_shape=out_shape,
        in_specs=in_specs,
        out_specs=out_specs,
        scratch_shapes=scratch,
        input_output_aliases=aliases,
        compiler_params=pltpu.CompilerParams(vmem_limit_bytes=mib * 1024 * 1024),
        cost_estimate=pl.CostEstimate(flops=0, bytes_accessed=0, transcendentals=0),
    )(*operands)


def mask_rows(place, flags, weight):
    masked = jax.ShapeDtypeStruct(weight.shape, weight.dtype)
    return local_call(
        mask_kernel, [masked] * 2, [place, flags, weight], [SMEM, VMEM, VMEM], [VMEM] * 2
    )


def split_columns(place, cot, whole):
    rows, columns = whole.shape
    piece = jax.ShapeDtypeStruct((rows, columns // SIDE + cot.shape[1]), whole.dtype)
    return local_call(
        split_kernel,
        [piece] * SIDE,
        [place, cot, whole],
        [SMEM, VMEM, HBM],
        [VMEM] * SIDE,
        [pltpu.SemaphoreType.DMA((SIDE, SIDE))],
    )


def join_columns(place, pieces, senders, whole=None):
    rows, columns = pieces[0].shape
    shape = jax.ShapeDtypeStruct((rows, columns * SIDE), pieces[0].dtype)
    chosen = [pieces[m] for m in senders]
    operands = [place, *chosen] + ([] if whole is None else [whole])
    specs = [SMEM] + [VMEM] * len(chosen) + ([] if whole is None else [HBM])
    return local_call(
        functools.partial(join_kernel, senders),
        [shape],
        operands,
        specs,
        [HBM],
        [pltpu.SemaphoreType.DMA((len(senders), SIDE))],
        aliases={} if whole is None else {len(operands) - 1: 0},
    )[0]


def layer_term(cots, rows, j):
    tokens, features = cots.shape[0] // SIDE, cots.shape[1]
    width = rows[0].shape[0]
    out = jax.ShapeDtypeStruct((tokens, SIDE * width), jnp.bfloat16)
    flops = 2 * tokens * features * width * SIDE
    return local_call(
        functools.partial(layer_kernel, j),
        [out],
        [cots, *rows],
        [VMEM] * (1 + len(rows)),
        [VMEM],
        (),
        flops,
    )[0]


def weight_term(ins, cots, m):
    tokens, features = cots.shape
    width = (ins[0].shape[1] - features) // SIDE
    coded = m != 0
    part = jax.ShapeDtypeStruct((width + (TAIL if coded else 0), features), jnp.float32)
    kernel = functools.partial(weight_kernel, m, coded)
    flops = 2 * tokens * features * width
    part = local_call(kernel, [part], [*ins, cots], [VMEM] * (SIDE + 1), [VMEM], (), flops)[0]
    return part.astype(jnp.float16) if coded else part


def exchange(pieces, first):
    received = [pieces[0]]
    for j in range(1, SIDE):
        with jax.named_scope(f"from{j}"):
            received.append(move(pieces[-j % SIDE], first, -j))
    return received


def after(value, *others):
    return lax.optimization_barrier((value, others))[0]


def decoded(value):
    return value[:-TAIL].astype(jnp.float32) * jnp.exp2(-value[-1:, :1].astype(jnp.float32))


def shards(layer_input, key_cotangent, key_weight, block_mask):
    inputs = layer_input[0]
    cotangent = key_cotangent[0]
    weight = key_weight[0]
    own_index = lax.axis_index("dp")
    parity = lax.axis_index("section") % 2
    x, y = own_index // SIDE, own_index % SIDE
    place = jnp.where(
        parity == 0, jnp.stack([0, x, y, own_index]), jnp.stack([1, y, x, own_index])
    ).astype(jnp.int32)
    features = cotangent.shape[1]

    pieces = list(split_columns(place, cotangent, inputs))
    masked, mask = mask_rows(place, block_mask[0].T, after(weight, pieces[0]))
    with jax.named_scope("rows_below"):
        rows_above = to_layer_below(masked)

    pieces[2], rows_above = lax.optimization_barrier((pieces[2], rows_above))
    with jax.named_scope("ins"):
        ins = exchange(pieces, True)
    cots = jnp.concatenate([piece[:, -features:] for piece in ins], 0)
    with jax.named_scope("cots_below"):
        cots_above = to_layer_below(cots)
    with jax.named_scope("rows"):
        far = after(rows_above, ins[1], ins[3])
        rows = exchange([rows_above, rows_above, far, rows_above], True)

    ins, cots, rows[1], rows[3] = lax.optimization_barrier((ins, cots, rows[1], rows[3]))
    parts = [None] * SIDE
    with jax.named_scope("weight"):
        parts[2] = weight_term(ins, cots, 2)
        parts[1] = weight_term(after(ins, parts[2]), cots, 1)
        parts[3] = weight_term(after(ins, parts[1]), cots, 3)

    parts[1], parts[2], parts[3], rows[2] = lax.optimization_barrier((*parts[1:], rows[2]))

    terms = [None] * SIDE
    with jax.named_scope("layer"):
        terms[1] = layer_term(cots_above, rows, 1)
        terms[3] = layer_term(after(cots_above, terms[1]), rows, 3)
        terms[2] = layer_term(after(cots_above, terms[3]), rows, 2)
        terms[0] = layer_term(after(cots_above, terms[2]), rows, 0)
        grads = exchange(terms, False)
    with jax.named_scope("join"):
        input_grad = join_columns(place, grads, (0, 1, 2, 3))

    with jax.named_scope("weight"):
        parts[0] = weight_term(after(ins, terms), cots, 0)
        sent = after(exchange(parts, False), terms)
        total = sent[0]
        for value in sent[1:]:
            total = lax.optimization_barrier(total + decoded(value))
        grad_scale = 1.0 / math.sqrt(cotangent.shape[0] * lax.axis_size("dp"))
        weight_grad = total * (mask.astype(jnp.float32) * grad_scale)
    return (weight_grad[None], input_grad[None])


def solution(mesh):
    placed = (
        P("section", "dp", None),
        P("section", "dp", None),
        P("section", "dp", None),
        P("section", None, None),
    )
    return jax.shard_map(
        shards,
        mesh=mesh,
        in_specs=placed,
        out_specs=(P("section", "dp", None), P("section", "dp", None)),
        check_vma=False,
    )
```

```python
import functools
import math

import jax
import jax.numpy as jnp
from jax import lax
from jax.experimental import pallas as pl
from jax.experimental.pallas import tpu as pltpu
from jax.sharding import PartitionSpec as P

BLOCK = 64
SIDE = 4
TAIL = 8
VMEM = pl.BlockSpec(memory_space=pltpu.VMEM)
SMEM = pl.BlockSpec(memory_space=pltpu.SMEM)
HBM = pl.BlockSpec(memory_space=pltpu.HBM)


def on_axis(index, parity, first, steps):
    x, y = index // SIDE, index % SIDE
    if (parity == 0) == first:
        x = (x + steps) % SIDE
    else:
        y = (y + steps) % SIDE
    return x * SIDE + y


def move(value, first, steps):
    sections, replicas = lax.axis_size("section"), lax.axis_size("dp")
    pairs = [
        (s * replicas + i, s * replicas + on_axis(i, s % 2, first, steps))
        for s in range(sections)
        for i in range(replicas)
    ]
    return lax.ppermute(value, ("section", "dp"), pairs)


def to_layer_below(value):
    count = lax.axis_size("section")
    return lax.ppermute(value, "section", [(s, s - 1) for s in range(1, count)])


def column_start(place_ref, k, m, width):
    a = lax.rem(place_ref[1] + k, SIDE)
    b = lax.rem(place_ref[2] + m, SIDE)
    owner = jnp.where(place_ref[0] == 0, a * SIDE + b, b * SIDE + a)
    return pl.multiple_of(owner * width, width)


def mask_kernel(place_ref, flags_ref, weight_ref, masked_ref, mask_ref):
    rows, columns = weight_ref.shape
    block_columns, all_block_rows = flags_ref.shape
    first = place_ref[3] * (rows // BLOCK)

    def spread(short, long, offset):
        block = lax.broadcasted_iota(jnp.int32, (short, long), 1) // BLOCK + offset
        return (block == lax.broadcasted_iota(jnp.int32, (short, long), 0)).astype(jnp.float32)

    tall = jnp.dot(
        flags_ref[...].astype(jnp.float32),
        spread(all_block_rows, rows, first),
        preferred_element_type=jnp.float32,
    )
    mask = lax.dot_general(
        tall,
        spread(block_columns, columns, 0),
        (((0,), (0,)), ((), ())),
        preferred_element_type=jnp.float32,
    ).astype(jnp.bfloat16)
    mask_ref[...] = mask
    masked_ref[...] = weight_ref[...] * mask


def split_kernel(place_ref, cot_ref, whole_ref, *refs):
    pieces, sem = refs[:SIDE], refs[SIDE]
    features = cot_ref.shape[1]
    width = (pieces[0].shape[1] - features) // SIDE
    copies = []
    for k in (2, 1, 3, 0):
        for m in range(SIDE):
            start = column_start(place_ref, k, m, width)
            copies.append(
                pltpu.make_async_copy(
                    whole_ref.at[:, pl.ds(start, width)],
                    pieces[k].at[:, pl.ds(m * width, width)],
                    sem.at[k, m],
                )
            )
    for copy in copies:
        copy.start()
    for piece in pieces:
        piece[:, SIDE * width :] = cot_ref[...]
    for copy in copies:
        copy.wait()


def join_kernel(senders, place_ref, *refs):
    pieces, whole_ref, sem = refs[: len(senders)], refs[-2], refs[-1]
    width = pieces[0].shape[1] // SIDE
    copies = []
    for n, m in enumerate(senders):
        for k in range(SIDE):
            start = column_start(place_ref, k, m, width)
            copies.append(
                pltpu.make_async_copy(
                    pieces[n].at[:, pl.ds(k * width, width)],
                    whole_ref.at[:, pl.ds(start, width)],
                    sem.at[n, k],
                )
            )
    for copy in copies:
        copy.start()
    for copy in copies:
        copy.wait()


def layer_kernel(j, cots_ref, *refs):
    rows, out_ref = refs[:-1], refs[-1]
    tokens = out_ref.shape[0]
    start = 0
    for row_ref in rows:
        stop = start + row_ref.shape[0]
        out_ref[:, start:stop] = lax.dot_general(
            cots_ref[j * tokens : (j + 1) * tokens, :],
            row_ref[...],
            (((1,), (1,)), ((), ())),
            preferred_element_type=jnp.float32,
        ).astype(jnp.bfloat16)
        start = stop


def weight_kernel(m, coded, *refs):
    ins, cots_ref, out_ref = refs[:SIDE], refs[SIDE], refs[SIDE + 1]
    features = out_ref.shape[1]
    width = (ins[0].shape[1] - features) // SIDE
    part = lax.dot_general(
        jnp.concatenate([i[:, m * width : (m + 1) * width] for i in ins], 0),
        cots_ref[...],
        (((0,), (0,)), ((), ())),
        preferred_element_type=jnp.float32,
    )
    if coded:
        peak = jnp.max(jnp.abs(part), axis=0, keepdims=True)
        peak = jnp.max(peak, axis=1, keepdims=True)
        exponent = jnp.clip(jnp.floor(14.0 - jnp.log2(peak)), -100.0, 100.0)
        out_ref[:width, :] = part * jnp.exp2(exponent)
        out_ref[width:, :] = jnp.broadcast_to(exponent, (TAIL, features))
    else:
        out_ref[...] = part


def local_call(
    kernel, out_shape, operands, in_specs, out_specs, scratch=(), flops=0, aliases={}, mib=40
):
    shapes = list(operands) + list(out_shape)
    moved = sum(math.prod(a.shape) * a.dtype.itemsize for a in shapes)
    return pl.pallas_call(
        kernel,
        out_shape=out_shape,
        in_specs=in_specs,
        out_specs=out_specs,
        scratch_shapes=scratch,
        input_output_aliases=aliases,
        compiler_params=pltpu.CompilerParams(vmem_limit_bytes=mib * 1024 * 1024),
        cost_estimate=pl.CostEstimate(flops=0, bytes_accessed=0, transcendentals=0),
    )(*operands)


def mask_rows(place, flags, weight):
    masked = jax.ShapeDtypeStruct(weight.shape, weight.dtype)
    return local_call(
        mask_kernel, [masked] * 2, [place, flags, weight], [SMEM, VMEM, VMEM], [VMEM] * 2
    )


def split_columns(place, cot, whole):
    rows, columns = whole.shape
    piece = jax.ShapeDtypeStruct((rows, columns // SIDE + cot.shape[1]), whole.dtype)
    return local_call(
        split_kernel,
        [piece] * SIDE,
        [place, cot, whole],
        [SMEM, VMEM, HBM],
        [VMEM] * SIDE,
        [pltpu.SemaphoreType.DMA((SIDE, SIDE))],
    )


def join_columns(place, pieces, senders, whole=None):
    rows, columns = pieces[0].shape
    shape = jax.ShapeDtypeStruct((rows, columns * SIDE), pieces[0].dtype)
    chosen = [pieces[m] for m in senders]
    operands = [place, *chosen] + ([] if whole is None else [whole])
    specs = [SMEM] + [VMEM] * len(chosen) + ([] if whole is None else [HBM])
    return local_call(
        functools.partial(join_kernel, senders),
        [shape],
        operands,
        specs,
        [HBM],
        [pltpu.SemaphoreType.DMA((len(senders), SIDE))],
        aliases={} if whole is None else {len(operands) - 1: 0},
    )[0]


def layer_term(cots, rows, j):
    tokens, features = cots.shape[0] // SIDE, cots.shape[1]
    width = rows[0].shape[0]
    out = jax.ShapeDtypeStruct((tokens, SIDE * width), jnp.bfloat16)
    flops = 2 * tokens * features * width * SIDE
    return local_call(
        functools.partial(layer_kernel, j),
        [out],
        [cots, *rows],
        [VMEM] * (1 + len(rows)),
        [VMEM],
        (),
        flops,
    )[0]


def weight_term(ins, cots, m):
    tokens, features = cots.shape
    width = (ins[0].shape[1] - features) // SIDE
    coded = m != 0
    part = jax.ShapeDtypeStruct((width + (TAIL if coded else 0), features), jnp.float32)
    kernel = functools.partial(weight_kernel, m, coded)
    flops = 2 * tokens * features * width
    part = local_call(kernel, [part], [*ins, cots], [VMEM] * (SIDE + 1), [VMEM], (), flops)[0]
    return part.astype(jnp.float16) if coded else part


def exchange(pieces, first):
    received = [pieces[0]]
    for j in range(1, SIDE):
        with jax.named_scope(f"from{j}"):
            received.append(move(pieces[-j % SIDE], first, -j))
    return received


def after(value, *others):
    return lax.optimization_barrier((value, others))[0]


def decoded(value):
    return value[:-TAIL].astype(jnp.float32) * jnp.exp2(-value[-1:, :1].astype(jnp.float32))


def shards(layer_input, key_cotangent, key_weight, block_mask):
    inputs = layer_input[0]
    cotangent = key_cotangent[0]
    weight = key_weight[0]
    own_index = lax.axis_index("dp")
    parity = lax.axis_index("section") % 2
    x, y = own_index // SIDE, own_index % SIDE
    place = jnp.where(
        parity == 0, jnp.stack([0, x, y, own_index]), jnp.stack([1, y, x, own_index])
    ).astype(jnp.int32)
    features = cotangent.shape[1]

    pieces = list(split_columns(place, cotangent, inputs))
    masked, mask = mask_rows(place, block_mask[0].T, after(weight, pieces[0]))
    with jax.named_scope("rows_below"):
        rows_above = to_layer_below(masked)

    with jax.named_scope("ins"):
        ins = exchange(pieces, True)
    cots = jnp.concatenate([piece[:, -features:] for piece in ins], 0)
    with jax.named_scope("cots_below"):
        cots_above = to_layer_below(cots)
    with jax.named_scope("rows"):
        rows = exchange([rows_above] * SIDE, True)

    parts = [None] * SIDE
    with jax.named_scope("weight"):
        parts[2] = weight_term(ins, cots, 2)
        parts[1] = weight_term(after(ins, parts[2]), cots, 1)
        parts[3] = weight_term(after(ins, parts[1]), cots, 3)

    parts[1:], rows = lax.optimization_barrier((parts[1:], rows))

    terms = [None] * SIDE
    with jax.named_scope("layer"):
        terms[1] = layer_term(cots_above, rows, 1)
        terms[3] = layer_term(after(cots_above, terms[1]), rows, 3)
        sent = exchange(parts, False)
        terms[2] = layer_term(after(cots_above, sent[1]), rows, 2)
        terms[0] = layer_term(after(cots_above, terms[2]), rows, 0)
        grads = exchange(terms, False)
    with jax.named_scope("join"):
        input_grad = join_columns(place, grads, (0, 1, 2, 3))

    with jax.named_scope("weight"):
        total = weight_term(after(ins, terms[3]), cots, 0)
        for value in after(sent[1:], terms):
            total = lax.optimization_barrier(total + decoded(value))
        grad_scale = 1.0 / math.sqrt(cotangent.shape[0] * lax.axis_size("dp"))
        weight_grad = total * (mask.astype(jnp.float32) * grad_scale)
    return (weight_grad[None], input_grad[None])


def solution(mesh):
    placed = (
        P("section", "dp", None),
        P("section", "dp", None),
        P("section", "dp", None),
        P("section", None, None),
    )
    return jax.shard_map(
        shards,
        mesh=mesh,
        in_specs=placed,
        out_specs=(P("section", "dp", None), P("section", "dp", None)),
        check_vma=False,
    )
```

```python
import functools
import math

import jax
import jax.numpy as jnp
from jax import lax
from jax.experimental import pallas as pl
from jax.experimental.pallas import tpu as pltpu
from jax.sharding import PartitionSpec as P

BLOCK = 64
SIDE = 4
TAIL = 8
VMEM = pl.BlockSpec(memory_space=pltpu.VMEM)
SMEM = pl.BlockSpec(memory_space=pltpu.SMEM)
HBM = pl.BlockSpec(memory_space=pltpu.HBM)


def on_axis(index, parity, first, steps):
    x, y = index // SIDE, index % SIDE
    if (parity == 0) == first:
        x = (x + steps) % SIDE
    else:
        y = (y + steps) % SIDE
    return x * SIDE + y


def move(value, first, steps):
    sections, replicas = lax.axis_size("section"), lax.axis_size("dp")
    pairs = [
        (s * replicas + i, s * replicas + on_axis(i, s % 2, first, steps))
        for s in range(sections)
        for i in range(replicas)
    ]
    return lax.ppermute(value, ("section", "dp"), pairs)


def to_layer_below(value):
    count = lax.axis_size("section")
    return lax.ppermute(value, "section", [(s, s - 1) for s in range(1, count)])


def column_start(place_ref, k, m, width):
    a = lax.rem(place_ref[1] + k, SIDE)
    b = lax.rem(place_ref[2] + m, SIDE)
    owner = jnp.where(place_ref[0] == 0, a * SIDE + b, b * SIDE + a)
    return pl.multiple_of(owner * width, width)


def mask_kernel(place_ref, flags_ref, weight_ref, masked_ref, mask_ref):
    rows, columns = weight_ref.shape
    block_columns, all_block_rows = flags_ref.shape
    first = place_ref[3] * (rows // BLOCK)

    def spread(short, long, offset):
        block = lax.broadcasted_iota(jnp.int32, (short, long), 1) // BLOCK + offset
        return (block == lax.broadcasted_iota(jnp.int32, (short, long), 0)).astype(jnp.float32)

    tall = jnp.dot(
        flags_ref[...].astype(jnp.float32),
        spread(all_block_rows, rows, first),
        preferred_element_type=jnp.float32,
    )
    mask = lax.dot_general(
        tall,
        spread(block_columns, columns, 0),
        (((0,), (0,)), ((), ())),
        preferred_element_type=jnp.float32,
    ).astype(jnp.bfloat16)
    mask_ref[...] = mask
    masked_ref[...] = weight_ref[...] * mask


def split_kernel(place_ref, cot_ref, whole_ref, *refs):
    pieces, sem = refs[:SIDE], refs[SIDE]
    features = cot_ref.shape[1]
    width = (pieces[0].shape[1] - features) // SIDE
    copies = []
    for k in (2, 1, 3, 0):
        for m in range(SIDE):
            start = column_start(place_ref, k, m, width)
            copies.append(
                pltpu.make_async_copy(
                    whole_ref.at[:, pl.ds(start, width)],
                    pieces[k].at[:, pl.ds(m * width, width)],
                    sem.at[k, m],
                )
            )
    for copy in copies:
        copy.start()
    for piece in pieces:
        piece[:, SIDE * width :] = cot_ref[...]
    for copy in copies:
        copy.wait()


def join_kernel(senders, place_ref, *refs):
    pieces, whole_ref, sem = refs[: len(senders)], refs[-2], refs[-1]
    width = pieces[0].shape[1] // SIDE
    copies = []
    for n, m in enumerate(senders):
        for k in range(SIDE):
            start = column_start(place_ref, k, m, width)
            copies.append(
                pltpu.make_async_copy(
                    pieces[n].at[:, pl.ds(k * width, width)],
                    whole_ref.at[:, pl.ds(start, width)],
                    sem.at[n, k],
                )
            )
    for copy in copies:
        copy.start()
    for copy in copies:
        copy.wait()


def layer_kernel(j, cots_ref, *refs):
    rows, out_ref = refs[:-1], refs[-1]
    tokens = out_ref.shape[0]
    start = 0
    for row_ref in rows:
        stop = start + row_ref.shape[0]
        out_ref[:, start:stop] = lax.dot_general(
            cots_ref[j * tokens : (j + 1) * tokens, :],
            row_ref[...],
            (((1,), (1,)), ((), ())),
            preferred_element_type=jnp.float32,
        ).astype(jnp.bfloat16)
        start = stop


def weight_kernel(m, coded, *refs):
    ins, cots_ref, outs = refs[:SIDE], refs[SIDE], refs[SIDE + 1 :]
    features = cots_ref.shape[1]
    width = (ins[0].shape[1] - features) // SIDE
    part = lax.dot_general(
        jnp.concatenate([i[:, m * width : (m + 1) * width] for i in ins], 0),
        cots_ref[...],
        (((0,), (0,)), ((), ())),
        preferred_element_type=jnp.float32,
    )
    if coded:
        peak = jnp.max(jnp.abs(part), axis=0, keepdims=True)
        peak = jnp.max(peak, axis=1, keepdims=True)
        exponent = jnp.clip(jnp.floor(14.0 - jnp.log2(peak)), -100.0, 100.0)
        rows = width // len(outs)
        for n, out_ref in enumerate(outs):
            out_ref[:rows, :] = part[n * rows : (n + 1) * rows] * jnp.exp2(exponent)
            out_ref[rows:, :] = jnp.broadcast_to(exponent, (TAIL, features))
    else:
        outs[0][...] = part


def local_call(
    kernel, out_shape, operands, in_specs, out_specs, scratch=(), flops=0, aliases={}, mib=40
):
    shapes = list(operands) + list(out_shape)
    moved = sum(math.prod(a.shape) * a.dtype.itemsize for a in shapes)
    return pl.pallas_call(
        kernel,
        out_shape=out_shape,
        in_specs=in_specs,
        out_specs=out_specs,
        scratch_shapes=scratch,
        input_output_aliases=aliases,
        compiler_params=pltpu.CompilerParams(vmem_limit_bytes=mib * 1024 * 1024),
        cost_estimate=pl.CostEstimate(flops=flops, bytes_accessed=0, transcendentals=0),
    )(*operands)


def mask_rows(place, flags, weight):
    masked = jax.ShapeDtypeStruct(weight.shape, weight.dtype)
    return local_call(
        mask_kernel, [masked] * 2, [place, flags, weight], [SMEM, VMEM, VMEM], [VMEM] * 2
    )


def split_columns(place, cot, whole):
    rows, columns = whole.shape
    piece = jax.ShapeDtypeStruct((rows, columns // SIDE + cot.shape[1]), whole.dtype)
    return local_call(
        split_kernel,
        [piece] * SIDE,
        [place, cot, whole],
        [SMEM, VMEM, HBM],
        [VMEM] * SIDE,
        [pltpu.SemaphoreType.DMA((SIDE, SIDE))],
    )


def join_columns(place, pieces, senders, whole=None):
    rows, columns = pieces[0].shape
    shape = jax.ShapeDtypeStruct((rows, columns * SIDE), pieces[0].dtype)
    chosen = [pieces[m] for m in senders]
    operands = [place, *chosen] + ([] if whole is None else [whole])
    specs = [SMEM] + [VMEM] * len(chosen) + ([] if whole is None else [HBM])
    return local_call(
        functools.partial(join_kernel, senders),
        [shape],
        operands,
        specs,
        [HBM],
        [pltpu.SemaphoreType.DMA((len(senders), SIDE))],
        aliases={} if whole is None else {len(operands) - 1: 0},
    )[0]


def layer_term(cots, rows, j):
    tokens, features = cots.shape[0] // SIDE, cots.shape[1]
    width = rows[0].shape[0]
    out = jax.ShapeDtypeStruct((tokens, SIDE * width), jnp.bfloat16)
    flops = 0
    return local_call(
        functools.partial(layer_kernel, j),
        [out],
        [cots, *rows],
        [VMEM] * (1 + len(rows)),
        [VMEM],
        (),
        flops,
    )[0]


def weight_term(ins, cots, m):
    tokens, features = cots.shape
    width = (ins[0].shape[1] - features) // SIDE
    coded = m != 0
    count = 2 if m == 2 else 1
    rows = width // count + (TAIL if coded else 0)
    parts = [jax.ShapeDtypeStruct((rows, features), jnp.float32)] * count
    kernel = functools.partial(weight_kernel, m, coded)
    flops = 16 * tokens * features * width
    return local_call(
        kernel, parts, [*ins, cots], [VMEM] * (SIDE + 1), [VMEM] * count, (), flops
    )


def exchange(pieces, first):
    received = [pieces[0]]
    for j in range(1, SIDE):
        with jax.named_scope(f"from{j}"):
            received.append(move(pieces[-j % SIDE], first, -j))
    return received


def after(value, *others):
    return lax.optimization_barrier((value, others))[0]


def decoded(value):
    return value[:-TAIL].astype(jnp.float32) * jnp.exp2(-value[-1:].astype(jnp.float32))


def combined(own, passed, first):
    rows = passed.shape[0] - TAIL
    own_exponent, passed_exponent = own[-1:], passed[-1:].astype(jnp.float32)
    exponent = jnp.minimum(own_exponent, passed_exponent) - 1.0
    own_scale = jnp.exp2(exponent - own_exponent)
    added = passed[:rows].astype(jnp.float32) * jnp.exp2(exponent - passed_exponent)
    top, bottom = own[:rows] * own_scale, own[rows : 2 * rows] * own_scale
    top, bottom = (top + added, bottom) if first else (top, bottom + added)
    tail = jnp.broadcast_to(exponent, (TAIL, own.shape[1]))
    return jnp.concatenate([top, bottom, tail], 0).astype(jnp.float16)


def shards(layer_input, key_cotangent, key_weight, block_mask):
    inputs = layer_input[0]
    cotangent = key_cotangent[0]
    weight = key_weight[0]
    own_index = lax.axis_index("dp")
    parity = lax.axis_index("section") % 2
    x, y = own_index // SIDE, own_index % SIDE
    place = jnp.where(
        parity == 0, jnp.stack([0, x, y, own_index]), jnp.stack([1, y, x, own_index])
    ).astype(jnp.int32)
    features = cotangent.shape[1]

    pieces = list(split_columns(place, cotangent, inputs))
    masked, mask = mask_rows(place, block_mask[0].T, after(weight, pieces[0]))
    with jax.named_scope("rows_below"):
        rows_above = to_layer_below(masked)

    with jax.named_scope("ins"):
        ins = exchange(pieces, True)
    cots = jnp.concatenate([piece[:, -features:] for piece in ins], 0)
    with jax.named_scope("cots_below"):
        cots_above = to_layer_below(cots)
    with jax.named_scope("rows"):
        before = move(rows_above, True, 1)
        behind = move(rows_above, True, -1)

    with jax.named_scope("weight"):
        halves = [part.astype(jnp.float16) for part in weight_term(ins, cots, 2)]
        (part_on,) = weight_term(after(ins, halves), cots, 1)
        (part_back,) = weight_term(after(ins, part_on), cots, 3)
    halves, part_on, part_back, before, behind = lax.optimization_barrier(
        (halves, part_on, part_back, before, behind)
    )
    with jax.named_scope("weight_far"):
        passed_on = move(halves[0], False, 1)
        passed_back = move(halves[1], False, -1)

    half = before.shape[0] // 2
    with jax.named_scope("rows_far"):
        far = [move(before[:half], True, 1), move(behind[half:], True, -1)]
    part_on, part_back, far, cots_above = lax.optimization_barrier(
        (part_on, part_back, far, cots_above)
    )
    rows = [rows_above, behind, *far, before]
    with jax.named_scope("weight_near"):
        sent = [
            move(combined(part_on, passed_on, True), False, 1),
            move(combined(part_back, passed_back, False), False, -1),
        ]

    terms = [None] * SIDE
    with jax.named_scope("layer"):
        terms[1] = layer_term(cots_above, rows, 1)
        terms[3] = layer_term(after(cots_above, terms[1]), rows, 3)
        terms[2] = layer_term(after(cots_above, terms[3]), rows, 2)
        terms[0] = layer_term(after(cots_above, terms[2]), rows, 0)
        grads = exchange(terms, False)
    with jax.named_scope("weight"):
        (total,) = weight_term(after(ins, terms[2]), cots, 0)
        for value in after(sent, terms):
            total = lax.optimization_barrier(total + decoded(value))
        grad_scale = 1.0 / math.sqrt(cotangent.shape[0] * lax.axis_size("dp"))
        weight_grad = total * (mask.astype(jnp.float32) * grad_scale)
    with jax.named_scope("join"):
        grads = after(grads, weight_grad)
        input_grad = join_columns(place, grads, (0, 2))
        input_grad = join_columns(place, grads, (1, 3), input_grad)
    return (weight_grad[None], input_grad[None])


def solution(mesh):
    placed = (
        P("section", "dp", None),
        P("section", "dp", None),
        P("section", "dp", None),
        P("section", None, None),
    )
    return jax.shard_map(
        shards,
        mesh=mesh,
        in_specs=placed,
        out_specs=(P("section", "dp", None), P("section", "dp", None)),
        check_vma=False,
    )
```

```python
import functools
import math

import jax
import jax.numpy as jnp
from jax import lax
from jax.experimental import pallas as pl
from jax.experimental.pallas import tpu as pltpu
from jax.sharding import PartitionSpec as P

BLOCK = 64
SIDE = 4
TAIL = 8
VMEM = pl.BlockSpec(memory_space=pltpu.VMEM)
SMEM = pl.BlockSpec(memory_space=pltpu.SMEM)
HBM = pl.BlockSpec(memory_space=pltpu.HBM)


def on_axis(index, parity, first, steps):
    x, y = index // SIDE, index % SIDE
    if (parity == 0) == first:
        x = (x + steps) % SIDE
    else:
        y = (y + steps) % SIDE
    return x * SIDE + y


def move(value, first, steps):
    sections, replicas = lax.axis_size("section"), lax.axis_size("dp")
    pairs = [
        (s * replicas + i, s * replicas + on_axis(i, s % 2, first, steps))
        for s in range(sections)
        for i in range(replicas)
    ]
    return lax.ppermute(value, ("section", "dp"), pairs)


def to_layer_below(value):
    count = lax.axis_size("section")
    return lax.ppermute(value, "section", [(s, s - 1) for s in range(1, count)])


def column_start(place_ref, k, m, width):
    a = lax.rem(place_ref[1] + k, SIDE)
    b = lax.rem(place_ref[2] + m, SIDE)
    owner = jnp.where(place_ref[0] == 0, a * SIDE + b, b * SIDE + a)
    return pl.multiple_of(owner * width, width)


def mask_kernel(place_ref, flags_ref, weight_ref, masked_ref, mask_ref):
    rows, columns = weight_ref.shape
    block_columns, all_block_rows = flags_ref.shape
    first = place_ref[3] * (rows // BLOCK)

    def spread(short, long, offset):
        block = lax.broadcasted_iota(jnp.int32, (short, long), 1) // BLOCK + offset
        return (block == lax.broadcasted_iota(jnp.int32, (short, long), 0)).astype(jnp.float32)

    tall = jnp.dot(
        flags_ref[...].astype(jnp.float32),
        spread(all_block_rows, rows, first),
        preferred_element_type=jnp.float32,
    )
    mask = lax.dot_general(
        tall,
        spread(block_columns, columns, 0),
        (((0,), (0,)), ((), ())),
        preferred_element_type=jnp.float32,
    ).astype(jnp.bfloat16)
    mask_ref[...] = mask
    masked_ref[...] = weight_ref[...] * mask


def split_kernel(place_ref, cot_ref, whole_ref, *refs):
    pieces, sem = refs[:SIDE], refs[SIDE]
    features = cot_ref.shape[1]
    width = (pieces[0].shape[1] - features) // SIDE
    copies = []
    for k in (2, 1, 3, 0):
        for m in range(SIDE):
            start = column_start(place_ref, k, m, width)
            copies.append(
                pltpu.make_async_copy(
                    whole_ref.at[:, pl.ds(start, width)],
                    pieces[k].at[:, pl.ds(m * width, width)],
                    sem.at[k, m],
                )
            )
    for copy in copies:
        copy.start()
    for piece in pieces:
        piece[:, SIDE * width :] = cot_ref[...]
    for copy in copies:
        copy.wait()


def join_kernel(senders, place_ref, *refs):
    pieces, whole_ref, sem = refs[: len(senders)], refs[-2], refs[-1]
    width = pieces[0].shape[1] // SIDE
    copies = []
    for n, m in enumerate(senders):
        for k in range(SIDE):
            start = column_start(place_ref, k, m, width)
            copies.append(
                pltpu.make_async_copy(
                    pieces[n].at[:, pl.ds(k * width, width)],
                    whole_ref.at[:, pl.ds(start, width)],
                    sem.at[n, k],
                )
            )
    for copy in copies:
        copy.start()
    for copy in copies:
        copy.wait()


def layer_kernel(j, cots_ref, *refs):
    rows, out_ref = refs[:-1], refs[-1]
    tokens = out_ref.shape[0]
    start = 0
    for row_ref in rows:
        stop = start + row_ref.shape[0]
        out_ref[:, start:stop] = lax.dot_general(
            cots_ref[j * tokens : (j + 1) * tokens, :],
            row_ref[...],
            (((1,), (1,)), ((), ())),
            preferred_element_type=jnp.float32,
        ).astype(jnp.bfloat16)
        start = stop


def weight_kernel(m, coded, *refs):
    ins, cots_ref, outs = refs[:SIDE], refs[SIDE], refs[SIDE + 1 :]
    features = cots_ref.shape[1]
    width = (ins[0].shape[1] - features) // SIDE
    part = lax.dot_general(
        jnp.concatenate([i[:, m * width : (m + 1) * width] for i in ins], 0),
        cots_ref[...],
        (((0,), (0,)), ((), ())),
        preferred_element_type=jnp.float32,
    )
    if coded:
        peak = jnp.max(jnp.abs(part), axis=0, keepdims=True)
        peak = jnp.max(peak, axis=1, keepdims=True)
        exponent = jnp.clip(jnp.floor(14.0 - jnp.log2(peak)), -100.0, 100.0)
        rows = width // len(outs)
        for n, out_ref in enumerate(outs):
            out_ref[:rows, :] = part[n * rows : (n + 1) * rows] * jnp.exp2(exponent)
            out_ref[rows:, :] = jnp.broadcast_to(exponent, (TAIL, features))
    else:
        outs[0][...] = part


def local_call(
    kernel, out_shape, operands, in_specs, out_specs, scratch=(), flops=0, aliases={}, mib=40
):
    shapes = list(operands) + list(out_shape)
    moved = sum(math.prod(a.shape) * a.dtype.itemsize for a in shapes)
    return pl.pallas_call(
        kernel,
        out_shape=out_shape,
        in_specs=in_specs,
        out_specs=out_specs,
        scratch_shapes=scratch,
        input_output_aliases=aliases,
        compiler_params=pltpu.CompilerParams(vmem_limit_bytes=mib * 1024 * 1024),
        cost_estimate=pl.CostEstimate(flops=flops, bytes_accessed=0, transcendentals=0),
    )(*operands)


def mask_rows(place, flags, weight):
    masked = jax.ShapeDtypeStruct(weight.shape, weight.dtype)
    return local_call(
        mask_kernel, [masked] * 2, [place, flags, weight], [SMEM, VMEM, VMEM], [VMEM] * 2
    )


def split_columns(place, cot, whole):
    rows, columns = whole.shape
    piece = jax.ShapeDtypeStruct((rows, columns // SIDE + cot.shape[1]), whole.dtype)
    return local_call(
        split_kernel,
        [piece] * SIDE,
        [place, cot, whole],
        [SMEM, VMEM, HBM],
        [VMEM] * SIDE,
        [pltpu.SemaphoreType.DMA((SIDE, SIDE))],
    )


def join_columns(place, pieces, senders, whole=None):
    rows, columns = pieces[0].shape
    shape = jax.ShapeDtypeStruct((rows, columns * SIDE), pieces[0].dtype)
    chosen = [pieces[m] for m in senders]
    operands = [place, *chosen] + ([] if whole is None else [whole])
    specs = [SMEM] + [VMEM] * len(chosen) + ([] if whole is None else [HBM])
    return local_call(
        functools.partial(join_kernel, senders),
        [shape],
        operands,
        specs,
        [HBM],
        [pltpu.SemaphoreType.DMA((len(senders), SIDE))],
        aliases={} if whole is None else {len(operands) - 1: 0},
    )[0]


def layer_term(cots, rows, j):
    tokens, features = cots.shape[0] // SIDE, cots.shape[1]
    width = rows[0].shape[0]
    out = jax.ShapeDtypeStruct((tokens, SIDE * width), jnp.bfloat16)
    flops = 0
    return local_call(
        functools.partial(layer_kernel, j),
        [out],
        [cots, *rows],
        [VMEM] * (1 + len(rows)),
        [VMEM],
        (),
        flops,
    )[0]


def weight_term(ins, cots, m):
    tokens, features = cots.shape
    width = (ins[0].shape[1] - features) // SIDE
    coded = m != 0
    count = 2 if m == 2 else 1
    rows = width // count + (TAIL if coded else 0)
    parts = [jax.ShapeDtypeStruct((rows, features), jnp.float32)] * count
    kernel = functools.partial(weight_kernel, m, coded)
    flops = 16 * tokens * features * width
    return local_call(
        kernel, parts, [*ins, cots], [VMEM] * (SIDE + 1), [VMEM] * count, (), flops
    )


def exchange(pieces, first):
    received = [pieces[0]]
    for j in range(1, SIDE):
        with jax.named_scope(f"from{j}"):
            received.append(move(pieces[-j % SIDE], first, -j))
    return received


def after(value, *others):
    return lax.optimization_barrier((value, others))[0]


def decoded(value):
    return value[:-TAIL].astype(jnp.float32) * jnp.exp2(-value[-1:].astype(jnp.float32))


def combined(own, passed, first):
    rows = passed.shape[0] - TAIL
    own_exponent, passed_exponent = own[-1:], passed[-1:].astype(jnp.float32)
    exponent = jnp.minimum(own_exponent, passed_exponent) - 1.0
    own_scale = jnp.exp2(exponent - own_exponent)
    added = passed[:rows].astype(jnp.float32) * jnp.exp2(exponent - passed_exponent)
    top, bottom = own[:rows] * own_scale, own[rows : 2 * rows] * own_scale
    top, bottom = (top + added, bottom) if first else (top, bottom + added)
    tail = jnp.broadcast_to(exponent, (TAIL, own.shape[1]))
    return jnp.concatenate([top, bottom, tail], 0).astype(jnp.float16)


def shards(layer_input, key_cotangent, key_weight, block_mask):
    inputs = layer_input[0]
    cotangent = key_cotangent[0]
    weight = key_weight[0]
    own_index = lax.axis_index("dp")
    parity = lax.axis_index("section") % 2
    x, y = own_index // SIDE, own_index % SIDE
    place = jnp.where(
        parity == 0, jnp.stack([0, x, y, own_index]), jnp.stack([1, y, x, own_index])
    ).astype(jnp.int32)
    features = cotangent.shape[1]

    pieces = list(split_columns(place, cotangent, inputs))
    masked, mask = mask_rows(place, block_mask[0].T, after(weight, pieces[0]))
    with jax.named_scope("rows_below"):
        rows_above = to_layer_below(masked)

    with jax.named_scope("ins"):
        ins = exchange(pieces, True)
    cots = jnp.concatenate([piece[:, -features:] for piece in ins], 0)
    with jax.named_scope("cots_below"):
        cots_above = to_layer_below(cots)
    with jax.named_scope("rows"):
        before = move(rows_above, True, 1)
        behind = move(rows_above, True, -1)

    with jax.named_scope("weight"):
        halves = [part.astype(jnp.float16) for part in weight_term(ins, cots, 2)]
        (part_on,) = weight_term(after(ins, halves), cots, 1)
        (part_back,) = weight_term(after(ins, part_on), cots, 3)
    halves, part_on, part_back, before, behind = lax.optimization_barrier(
        (halves, part_on, part_back, before, behind)
    )
    with jax.named_scope("weight_far"):
        passed_on = move(halves[0], False, 1)
        passed_back = move(halves[1], False, -1)

    half = before.shape[0] // 2
    with jax.named_scope("rows_far"):
        far = [move(before[:half], True, 1), move(behind[half:], True, -1)]
    part_on, part_back, far, cots_above = lax.optimization_barrier(
        (part_on, part_back, far, cots_above)
    )
    rows = [rows_above, behind, *far, before]
    with jax.named_scope("weight_near"):
        sent = [
            move(combined(part_on, passed_on, True), False, 1),
            move(combined(part_back, passed_back, False), False, -1),
        ]

    terms = [None] * SIDE
    with jax.named_scope("layer"):
        terms[1] = layer_term(cots_above, rows, 1)
        terms[3] = layer_term(after(cots_above, terms[1]), rows, 3)
        terms[2] = layer_term(after(cots_above, terms[3]), rows, 2)
        terms[0] = layer_term(after(cots_above, terms[2]), rows, 0)
        grads = exchange(terms, False)
    with jax.named_scope("weight"):
        (total,) = weight_term(after(ins, terms[2]), cots, 0)
        for value in after(sent, terms):
            total = lax.optimization_barrier(total + decoded(value))
        grad_scale = 1.0 / math.sqrt(cotangent.shape[0] * lax.axis_size("dp"))
        weight_grad = total * (mask.astype(jnp.float32) * grad_scale)
    with jax.named_scope("join"):
        grads = after(grads, weight_grad)
        input_grad = join_columns(place, grads, (0, 1, 2, 3))
    return (weight_grad[None], input_grad[None])


def solution(mesh):
    placed = (
        P("section", "dp", None),
        P("section", "dp", None),
        P("section", "dp", None),
        P("section", None, None),
    )
    return jax.shard_map(
        shards,
        mesh=mesh,
        in_specs=placed,
        out_specs=(P("section", "dp", None), P("section", "dp", None)),
        check_vma=False,
    )
```
